32 devices in a mesh: dp: 4 (over z), row: 2 (over x), col: 4 (over y, core).
Axes of the slice: x: 2, y: 2, z: 4, core: 2. Of those that a mesh axis runs over, the one named last changes fastest.
Arguments:
- tokens: bfloat16 [8192, 1024], P(('dp', 'row'), 'col'), may hold values from -6 to 6
- lengths: int32 [4, 9], P('dp'), may hold values from 1 to 512, as said below
- ln1_gain: bfloat16 [1024], P('col'), may hold values from 0.5 to 1.5
- ln1_bias: bfloat16 [1024], P('col'), may hold values from -3 to 3
- qkv_weight: bfloat16 [1024, 3, 1024], P('col', None, 'row'), may hold values from -0.1875 to 0.1875
- qv_bias: bfloat16 [2, 1024], P(None, ('row', 'col')), may hold values from -3 to 3
- out_weight: bfloat16 [1024, 1024], P('row', 'col'), may hold values from -0.5 to 0.5
- out_bias: bfloat16 [1024], P('col'), may hold values from -3 to 3
- ln2_gain: bfloat16 [1024], P('col'), may hold values from 0.5 to 1.5
- ln2_bias: bfloat16 [1024], P('col'), may hold values from -3 to 3
- up_weight: bfloat16 [1024, 4096], P('col', 'row'), may hold values from -0.1875 to 0.1875
- up_bias: bfloat16 [4096], P(('row', 'col')), may hold values from -3 to 3
- down_weight: bfloat16 [4096, 1024], P('row', 'col'), may hold values from -0.09375 to 0.09375
- down_bias: bfloat16 [1024], P('col'), may hold values from -3 to 3
- cotangent: bfloat16 [8192, 1024], P(('dp', 'row'), 'col'), may hold values from -6 to 6
Outputs:
- block_out: bfloat16 [8192, 1024], P(('dp', 'row'), 'col')
- grad_tokens: float32 [8192, 1024], P(('dp', 'row'), 'col')
- grad_ln1_gain: float32 [1024], P('col')
- grad_ln1_bias: float32 [1024], P('col')
- grad_qkv_weight: float32 [1024, 3, 1024], P('col', None, 'row')
- grad_qv_bias: float32 [2, 1024], P(None, ('row', 'col'))
- grad_out_weight: float32 [1024, 1024], P('row', 'col')
- grad_out_bias: float32 [1024], P('col')
- grad_ln2_gain: float32 [1024], P('col')
- grad_ln2_bias: float32 [1024], P('col')
- grad_up_weight: float32 [1024, 4096], P('col', 'row')
- grad_up_bias: float32 [4096], P(('row', 'col'))
- grad_down_weight: float32 [4096, 1024], P('row', 'col')
- grad_down_bias: float32 [1024], P('col')
The draws below stay inside these ranges and needn't reach their ends.
Inputs may be any that keep to these rules, and one draw needn't show every extreme that they name: Row g holds the lengths of the 9 sequences packed in order into the 2048 tokens of dp group g; they sum to 2048, and the longest of each row is exactly 512.
All inputs are finite; a program needn't handle non-finite values.
Results may differ from the reference program's by a relative error of at most 0.014.
Values may be sent and summed in bfloat16 or wider, within the bound.
A program may use at most 192 MiB of HBM per device.

```python
import math
import jax
import jax.numpy as jnp
from jax import lax

D = 1024
FF = 4096
HD = 64
HEADS = 16
TOK_G = 2048
MAXLEN = 512
TOKENS = 8192
N_DP = 4


def split_four(subkey, total):
    base_len = total // 4
    raw_bits = jax.random.randint(subkey, (N_DP, 4), 0, 1 << 20)
    wobble = raw_bits % (base_len // 2 + 1)[:, None]
    pieces = base_len[:, None] + wobble - jnp.roll(wobble, -1, axis=1)
    remainder = total - 4 * base_len
    return pieces.at[:, 0].add(remainder)


def draw_lengths(key, part):
    key = jax.random.fold_in(key, 11)
    first_key, second_key, third_key = jax.random.split(key, 3)
    offset_len = jax.random.randint(first_key, (N_DP,), 1, MAXLEN)
    before = TOK_G // 2 - offset_len
    after = TOK_G - before - MAXLEN
    longest = jnp.full((N_DP, 1), MAXLEN, jnp.int32)
    joined = jnp.concatenate([split_four(second_key, before), longest, split_four(third_key, after)], axis=1)
    return joined.astype(jnp.int32)


def levels(rng, dims, cuts, least, top_value):
    loudness, own = 1.0, jax.random.fold_in(rng, 6)
    for dim, parts in cuts:
        draws = jnp.exp(jax.random.uniform(jax.random.fold_in(own, dim), (parts,), jnp.float32, least / len(cuts), top_value / len(cuts)))
        loudness = loudness * jnp.repeat(draws, dims[dim] // parts).reshape([-1 if axis == dim else 1 for axis in range(len(dims))])
    return loudness


def normal_values(stream_key, dims, width, reach, cuts=(), kind=jnp.bfloat16):
    array = jax.random.normal(stream_key, dims, jnp.float32) * width
    if len(cuts) > 0:
        array = levels(stream_key, dims, cuts, -0.22, 0.18) * array
    return jnp.clip(array, min=-reach, max=reach).astype(kind)


def setup_inputs(seed: int = 0) -> dict:
    key_of = jax.random.split(jax.random.key(seed), 16)
    tokens = normal_values(key_of[0], (TOKENS, D), 1.0, 6.0, ((0, 8), (1, 4)))
    lengths = draw_lengths(jax.random.fold_in(key_of[15], 71), 0)
    ln1_gain = jnp.clip(1.0 + 0.1 * jax.random.normal(key_of[2], (D,), jnp.float32), 0.5, 1.5).astype(jnp.bfloat16)
    ln1_bias = normal_values(key_of[3], (D,), 0.3, 3.0, ((0, 4),))
    qkv_weight = normal_values(key_of[4], (D, 3, D), D ** -0.5, 0.1875, ((0, 4), (2, 2)))
    qv_bias = normal_values(key_of[5], (2, D), 0.3, 3.0, ((1, 8),))
    out_weight = normal_values(key_of[6], (D, D), (D // 8) ** -0.5, 0.5, ((0, 2), (1, 4)))
    out_bias = normal_values(key_of[7], (D,), 0.3, 3.0, ((0, 4),))
    ln2_gain = jnp.clip(1.0 + 0.1 * jax.random.normal(key_of[8], (D,), jnp.float32), 0.5, 1.5).astype(jnp.bfloat16)
    ln2_bias = normal_values(key_of[9], (D,), 0.3, 3.0, ((0, 4),))
    up_weight = normal_values(key_of[10], (D, FF), D ** -0.5, 0.1875, ((0, 4), (1, 2)))
    up_bias = normal_values(key_of[11], (FF,), 0.3, 3.0, ((0, 8),))
    down_weight = normal_values(key_of[12], (FF, D), FF ** -0.5, 0.09375, ((0, 2), (1, 4)))
    down_bias = normal_values(key_of[13], (D,), 0.3, 3.0, ((0, 4),))
    cotangent = normal_values(key_of[14], (TOKENS, D), 1.0, 6.0, ((0, 8), (1, 4)))
    return dict(tokens=tokens, lengths=lengths, ln1_gain=ln1_gain, ln1_bias=ln1_bias, qkv_weight=qkv_weight, qv_bias=qv_bias, out_weight=out_weight, out_bias=out_bias, ln2_gain=ln2_gain, ln2_bias=ln2_bias, up_weight=up_weight, up_bias=up_bias, down_weight=down_weight, down_bias=down_bias, cotangent=cotangent)


@jax.custom_vjp
def low(v):
    return lax.optimization_barrier(v.astype(jnp.bfloat16)).astype(jnp.float32)

@jax.custom_vjp
def low_back(v):
    return v

def low_keep(v):
    return (low(v), None)

def low_pass(kept, grad):
    return (grad,)

def back_keep(v):
    return (v, None)

def back_low(kept, grad):
    return (low(grad),)
low.defvjp(low_keep, low_pass)
low_back.defvjp(back_keep, back_low)

def layer_norm(values, gain, shift):
    mean = lax.optimization_barrier(jnp.mean(values, axis=-1, keepdims=True))
    centred = values - mean
    variance = lax.optimization_barrier(jnp.mean(centred * centred, axis=-1, keepdims=True))
    return centred * lax.rsqrt(variance + 1e-05) * gain + shift

def product(left, right):
    return jnp.dot(left, right, precision=lax.Precision.HIGHEST)

def gelu_tanh(values):
    return jax.nn.gelu(values, approximate=True)

def group_block(params, group_tokens, group_lengths):
    ln1_gain, ln1_bias, qkv_weight, qv_bias, out_weight, out_bias, ln2_gain, ln2_bias, up_weight, up_bias, down_weight, down_bias = params
    count = group_tokens.shape[0]
    places = jnp.arange(count, dtype=jnp.int32)
    ends = jnp.cumsum(group_lengths)
    sequence = lax.optimization_barrier(jnp.sum((places[:, None] >= ends[None, :]).astype(jnp.int32), axis=1))
    normed_one = low(layer_norm(group_tokens, ln1_gain, ln1_bias))
    projected = jnp.einsum('td,dke->tke', normed_one, qkv_weight, precision=lax.Precision.HIGHEST)
    bias_three = jnp.stack([qv_bias[0], jnp.zeros_like(qv_bias[0]), qv_bias[1]])
    projected = low(low_back(projected + bias_three[None]))
    query = projected[:, 0].reshape(count, HEADS, HD).transpose(1, 0, 2)
    keys = projected[:, 1].reshape(count, HEADS, HD).transpose(1, 0, 2)
    values = projected[:, 2].reshape(count, HEADS, HD).transpose(1, 0, 2)
    slopes = jnp.exp2(-8.0 * (jnp.arange(HEADS, dtype=jnp.float32) + 1.0) / HEADS)
    scale = 1.0 / math.sqrt(HD)

    def one_head(pieces):
        head_query, head_keys, head_values, slope = pieces
        distance = (places[None, :] - places[:, None]).astype(jnp.float32)
        allowed = (sequence[:, None] == sequence[None, :]) & (places[None, :] <= places[:, None])
        scores = product(head_query, head_keys.T) * scale + slope * distance
        scores = low_back(jnp.where(allowed, scores, -1e+30))
        probability = jax.nn.softmax(scores, axis=-1)
        return product(low(probability), head_values)
    context = lax.map(jax.checkpoint(one_head), (query, keys, values, slopes))
    context = low(low_back(context.transpose(1, 0, 2).reshape(count, HEADS * HD)))
    middle = group_tokens + low_back(product(context, out_weight)) + out_bias
    normed_two = low(layer_norm(middle, ln2_gain, ln2_bias))
    hidden = low_back(product(normed_two, up_weight) + up_bias)
    activated = low(gelu_tanh(hidden))
    return middle + low_back(product(activated, down_weight)) + down_bias

def reference(tokens, lengths, ln1_gain, ln1_bias, qkv_weight, qv_bias, out_weight, out_bias, ln2_gain, ln2_bias, up_weight, up_bias, down_weight, down_bias, cotangent):
    params = tuple((weight_arg.astype(jnp.float32) for weight_arg in (ln1_gain, ln1_bias, qkv_weight, qv_bias, out_weight, out_bias, ln2_gain, ln2_bias, up_weight, up_bias, down_weight, down_bias)))

    def forward(weights, inputs):
        stacked = inputs.reshape(N_DP, TOK_G, D)

        def per_group(pieces):
            return jax.checkpoint(group_block)(weights, pieces[0], pieces[1])
        return lax.map(per_group, (stacked, lengths)).reshape(N_DP * TOK_G, D)
    output, pullback = jax.vjp(forward, params, tokens.astype(jnp.float32))
    grad_params, grad_inputs = pullback(cotangent.astype(jnp.float32))
    return (output.astype(jnp.bfloat16), grad_inputs, grad_params[0], grad_params[1], grad_params[2], grad_params[3], grad_params[4], grad_params[5], grad_params[6], grad_params[7], grad_params[8], grad_params[9], grad_params[10], grad_params[11])
```

```python
import functools
import math

import jax
import jax.numpy as jnp
from jax import lax
from jax.experimental import pallas as pl
from jax.experimental.pallas import tpu as pltpu
from jax.sharding import PartitionSpec as P

HD = 64
HEADS = 16
LONGEST = 512
BLOCK = 256

epsilon = 1e-05
masked = -1e30
GROUP = ("row", "col")
VMEM_LIMIT = 48 * 1024 * 1024


def gelu_tanh(values):
    return jax.nn.gelu(values, approximate=True)


def norm_stats(values):
    mean = jnp.mean(values, axis=-1, keepdims=True)
    away = values - mean
    inverse = lax.rsqrt(jnp.mean(away * away, axis=-1, keepdims=True) + epsilon)
    return away * inverse, inverse


def norm_apply(centred, gain, shift):
    normed = centred * gain.astype(jnp.float32) + shift.astype(jnp.float32)
    return normed.astype(jnp.bfloat16)


def norm_backward(upstream, centred, inverse, gain):
    scaled = upstream * gain.astype(jnp.float32)
    total = jnp.mean(scaled, axis=-1, keepdims=True)
    mixed = jnp.mean(scaled * centred, axis=-1, keepdims=True)
    back = inverse * (scaled - total - centred * mixed)
    return (back, jnp.sum(upstream * centred, axis=0), jnp.sum(upstream, axis=0))


def product(left, right):
    return jnp.dot(left, right, preferred_element_type=jnp.float32)


def product_flip(left, right):
    return lax.dot_general(left, right, (((1,), (1,)), ((), ())), preferred_element_type=jnp.float32)


def outer_sum(left, right):
    return lax.dot_general(left, right, (((0,), (0,)), ((), ())), preferred_element_type=jnp.float32)


def head_parts(q_ref, k_ref, v_ref, first, slope, head, start, begin, window, scale):
    lanes = slice(head * HD, (head + 1) * HD)
    query = q_ref[pl.ds(start, BLOCK), lanes]
    keys = k_ref[pl.ds(begin, window), lanes]
    values = v_ref[pl.ds(begin, window), lanes]
    scores = product_flip(query, keys) * scale
    rows_at = start + lax.broadcasted_iota(jnp.int32, (BLOCK, window), 0)
    keys_at = begin + lax.broadcasted_iota(jnp.int32, (BLOCK, window), 1)
    distance = keys_at - rows_at
    scores = scores + slope * distance.astype(jnp.float32)
    scores = jnp.where((distance <= 0) & (keys_at >= first), scores, masked)
    peak = jnp.max(scores, axis=-1, keepdims=True)
    spread = jnp.exp(scores - peak)
    total = jnp.sum(spread, axis=-1, keepdims=True)
    return query, keys, values, spread * (1.0 / total)


def attend_kernel(heads, window, scale, slopes_ref, first_ref, q_ref, k_ref, v_ref, out_ref):
    start = pl.multiple_of(pl.program_id(0) * BLOCK, BLOCK)
    begin = pl.multiple_of(jnp.maximum(start + BLOCK - window, 0), BLOCK)
    first = first_ref[pl.ds(start, BLOCK), :]
    parts = []
    for head in range(heads):
        _, _, values, probability = head_parts(
            q_ref, k_ref, v_ref, first, slopes_ref[head], head, start, begin, window, scale
        )
        parts.append(product(probability.astype(jnp.bfloat16), values))
    out_ref[pl.ds(start, BLOCK), :] = jnp.concatenate(parts, axis=1).astype(jnp.bfloat16)


def attend_back_kernel(
    heads, window, scale, slopes_ref, first_ref, q_ref, k_ref, v_ref, up_ref, out_ref, dk_ref, dv_ref
):
    step = pl.program_id(0)

    @pl.when(step == 0)
    def _():
        dk_ref[...] = jnp.zeros_like(dk_ref)
        dv_ref[...] = jnp.zeros_like(dv_ref)

    start = pl.multiple_of(step * BLOCK, BLOCK)
    begin = pl.multiple_of(jnp.maximum(start + BLOCK - window, 0), BLOCK)
    first = first_ref[pl.ds(start, BLOCK), :]
    grads = []
    key_grads = []
    value_grads = []
    for head in range(heads):
        query, keys, values, probability = head_parts(
            q_ref, k_ref, v_ref, first, slopes_ref[head], head, start, begin, window, scale
        )
        above = up_ref[pl.ds(start, BLOCK), head * HD : (head + 1) * HD]
        grad_prob = product_flip(above, values)
        centre = jnp.sum(probability * grad_prob, axis=-1, keepdims=True)
        grad_scores = (probability * (grad_prob - centre)).astype(jnp.bfloat16)
        grads.append(product(grad_scores, keys) * scale)
        key_grads.append(outer_sum(grad_scores, query) * scale)
        value_grads.append(outer_sum(probability.astype(jnp.bfloat16), above))
    width = heads * HD
    out_ref[pl.ds(start, BLOCK), 0:width] = jnp.concatenate(grads, axis=1).astype(jnp.bfloat16)
    dk_ref[pl.ds(begin, window), :] += jnp.concatenate(key_grads, axis=1)
    dv_ref[pl.ds(begin, window), :] += jnp.concatenate(value_grads, axis=1)

    @pl.when(step == pl.num_programs(0) - 1)
    def _():
        out_ref[:, width : 2 * width] = dk_ref[...].astype(jnp.bfloat16)
        out_ref[:, 2 * width : 3 * width] = dv_ref[...].astype(jnp.bfloat16)


def attention_specs(count, width):
    whole = pl.BlockSpec((count, width), lambda i: (0, 0))
    return [
        pl.BlockSpec(memory_space=pltpu.SMEM),
        pl.BlockSpec((count, 1), lambda i: (0, 0)),
        pl.BlockSpec((count, width), lambda i: (0, 0)),
        pl.BlockSpec((count, width), lambda i: (0, 1)),
        pl.BlockSpec((count, width), lambda i: (0, 2)),
    ], whole


def attend(projected, first, slopes, scale):
    count = projected.shape[0]
    width = projected.shape[1] // 3
    heads = width // HD
    window = min(LONGEST + BLOCK, count)
    specs, whole = attention_specs(count, width)
    area = heads * count * window
    return pl.pallas_call(
        functools.partial(attend_kernel, heads, window, scale),
        grid=(count // BLOCK,),
        in_specs=specs,
        out_specs=whole,
        out_shape=jax.ShapeDtypeStruct((count, width), jnp.bfloat16),
        compiler_params=pltpu.CompilerParams(vmem_limit_bytes=VMEM_LIMIT),
        cost_estimate=pl.CostEstimate(
            flops=4 * area * HD, bytes_accessed=8 * count * width, transcendentals=area
        ),
        name="attend",
    )(slopes, first, projected, projected, projected)


def attend_back(projected, first, slopes, scale, upstream):
    count = projected.shape[0]
    width = projected.shape[1] // 3
    heads = width // HD
    window = min(LONGEST + BLOCK, count)
    specs, whole = attention_specs(count, width)
    area = heads * count * window
    return pl.pallas_call(
        functools.partial(attend_back_kernel, heads, window, scale),
        grid=(count // BLOCK,),
        in_specs=specs + [whole],
        out_specs=pl.BlockSpec((count, 3 * width), lambda i: (0, 0)),
        out_shape=jax.ShapeDtypeStruct((count, 3 * width), jnp.bfloat16),
        scratch_shapes=[pltpu.VMEM((count, width), jnp.float32)] * 2,
        compiler_params=pltpu.CompilerParams(vmem_limit_bytes=VMEM_LIMIT),
        cost_estimate=pl.CostEstimate(
            flops=10 * area * HD, bytes_accessed=14 * count * width, transcendentals=area
        ),
        name="attend_back",
    )(slopes, first, projected, projected, projected, upstream)


def gather_group(shard):
    return lax.all_gather(shard, GROUP, axis=0, tiled=True)


def scatter_group(partial_sum):
    summed = lax.psum_scatter(
        partial_sum.astype(jnp.bfloat16), GROUP, scatter_dimension=0, tiled=True
    )
    return summed.astype(jnp.float32)


def take_columns(shard):
    return lax.all_to_all(shard, "col", split_axis=shard.ndim - 1, concat_axis=0, tiled=True)


def take_rows(shard):
    return lax.all_to_all(shard, "col", split_axis=0, concat_axis=1, tiled=True)


def gather_tokens(shard):
    rows, features = shard.shape
    cols = lax.axis_size("col")
    pieces = lax.all_gather(shard, GROUP, axis=0, tiled=False)
    pieces = pieces.reshape(lax.axis_size("row"), cols, rows, features)
    return pieces.transpose(0, 2, 1, 3).reshape(-1, cols * features)


def on_device(
    tokens,
    lengths,
    ln1_gain,
    ln1_bias,
    qkv_weight,
    qv_bias,
    out_weight,
    out_bias,
    ln2_gain,
    ln2_bias,
    up_weight,
    up_bias,
    down_weight,
    down_bias,
    cotangent,
):
    cols = lax.axis_size("col")
    rows = lax.axis_size("row")
    count = tokens.shape[0] * rows
    own = count // (rows * cols)
    place = lax.axis_index("row") * cols + lax.axis_index("col")
    local_heads = qkv_weight.shape[2] // cols // HD
    first_head = place * local_heads
    slopes = jnp.exp2(
        -8.0
        * (first_head + jnp.arange(local_heads, dtype=jnp.int32) + 1).astype(jnp.float32)
        / HEADS
    )
    scale = 1.0 / math.sqrt(HD)
    ends = jnp.cumsum(lengths[0])
    starts = ends - lengths[0]
    places = jnp.arange(count, dtype=jnp.int32)
    first = jnp.max(
        jnp.where(starts[None, :] <= places[:, None], starts[None, :], 0), axis=1, keepdims=True
    )

    vectors = jnp.stack([ln1_gain, ln1_bias, out_bias, ln2_gain, ln2_bias, down_bias])
    vectors = lax.all_gather(vectors, "col", axis=1, tiled=True)
    gain_one, shift_one, bias_out, gain_two, shift_two, bias_down = (vectors[i] for i in range(6))

    qkv_local = take_columns(qkv_weight).reshape(-1, 3 * local_heads * HD)
    out_local = take_rows(out_weight)
    up_local = take_columns(up_weight)
    down_local = take_rows(down_weight)

    all_tokens = gather_tokens(tokens)
    all_cotangent = gather_tokens(cotangent)

    def mine(array):
        return lax.dynamic_slice_in_dim(array, place * own, own, axis=0)

    centred_all, _ = norm_stats(all_tokens.astype(jnp.float32))
    normed_one = norm_apply(centred_all, gain_one, shift_one)
    residual = mine(all_tokens).astype(jnp.float32)
    upstream = mine(all_cotangent).astype(jnp.float32)
    bias_three = jnp.concatenate([qv_bias[0], jnp.zeros_like(qv_bias[0]), qv_bias[1]])
    projected = (product(normed_one, qkv_local) + bias_three.astype(jnp.float32)).astype(
        jnp.bfloat16
    )
    context = attend(projected, first, slopes, scale)
    attention_out = scatter_group(product(context, out_local))
    middle = residual + attention_out + bias_out.astype(jnp.float32)
    centred_two, inverse_two = norm_stats(middle)
    normed_two = gather_group(norm_apply(centred_two, gain_two, shift_two))
    hidden = product(normed_two, up_local) + up_bias.astype(jnp.float32)
    activated, gelu_pull = jax.vjp(gelu_tanh, hidden)
    activated = activated.astype(jnp.bfloat16)
    grad_active = product_flip(all_cotangent, down_local)
    grad_hidden = gelu_pull(grad_active)[0].astype(jnp.bfloat16)
    grad_normed_two = scatter_group(product_flip(grad_hidden, up_local))
    feed_out = scatter_group(product(activated, down_local))
    block_out = (middle + feed_out + bias_down.astype(jnp.float32)).astype(jnp.bfloat16)

    grad_up_bias = jnp.sum(grad_hidden.astype(jnp.float32), axis=0)
    grad_up = outer_sum(normed_two, grad_hidden).astype(jnp.bfloat16)
    grad_down = outer_sum(activated, all_cotangent).astype(jnp.bfloat16)
    grad_down_bias = jnp.sum(upstream, axis=0)

    back_two, grad_ln2_gain, grad_ln2_bias = norm_backward(
        grad_normed_two, centred_two, inverse_two, gain_two
    )
    grad_middle = upstream + back_two
    grad_out_bias = jnp.sum(grad_middle, axis=0)
    grad_attention = gather_group(grad_middle.astype(jnp.bfloat16))
    grad_context = product_flip(grad_attention, out_local).astype(jnp.bfloat16)
    grad_out = outer_sum(context, grad_attention).astype(jnp.bfloat16)
    grad_projected = attend_back(projected, first, slopes, scale, grad_context)
    summed = jnp.sum(grad_projected.astype(jnp.float32), axis=0).reshape(3, -1)
    grad_qv_bias = jnp.stack([summed[0], summed[2]])
    grad_normed_one = scatter_group(product_flip(grad_projected, qkv_local))
    grad_qkv = outer_sum(normed_one, grad_projected).astype(jnp.bfloat16)

    centred_one, inverse_one = norm_stats(residual)
    back_one, grad_ln1_gain, grad_ln1_bias = norm_backward(
        grad_normed_one, centred_one, inverse_one, gain_one
    )
    grad_tokens = grad_middle + back_one

    def to_columns(array):
        return lax.all_to_all(array, "col", split_axis=1, concat_axis=0, tiled=True)

    def dp_sum(array):
        return lax.psum(array.astype(jnp.bfloat16), "dp").astype(jnp.float32)

    grad_up_weight = dp_sum(lax.all_to_all(grad_up, "col", split_axis=0, concat_axis=1, tiled=True))
    grad_down_weight = dp_sum(to_columns(grad_down))
    grad_out_weight = dp_sum(to_columns(grad_out))
    width = local_heads * HD
    grad_qkv_weight = dp_sum(
        lax.all_to_all(
            grad_qkv.reshape(-1, 3, width), "col", split_axis=0, concat_axis=2, tiled=True
        )
    )
    biases = jnp.concatenate([grad_qv_bias.reshape(-1), grad_up_bias])
    biases = lax.psum(biases, "dp")
    vector_sums = lax.psum(
        jnp.stack(
            [grad_ln1_gain, grad_ln1_bias, grad_out_bias, grad_ln2_gain, grad_ln2_bias, grad_down_bias]
        ),
        ("dp", "row", "col"),
    )
    features = tokens.shape[1]
    vector_sums = lax.dynamic_slice_in_dim(
        vector_sums, lax.axis_index("col") * features, features, axis=1
    )
    return (
        to_columns(block_out),
        to_columns(grad_tokens),
        vector_sums[0],
        vector_sums[1],
        grad_qkv_weight,
        biases[: 2 * width].reshape(2, width),
        grad_out_weight,
        vector_sums[2],
        vector_sums[3],
        vector_sums[4],
        grad_up_weight,
        biases[2 * width :],
        grad_down_weight,
        vector_sums[5],
    )


def solution(mesh):
    return jax.shard_map(
        on_device,
        mesh=mesh,
        in_specs=(
            P(("dp", "row"), "col"),
            P("dp", None),
            P("col"),
            P("col"),
            P("col", None, "row"),
            P(None, ("row", "col")),
            P("row", "col"),
            P("col"),
            P("col"),
            P("col"),
            P("col", "row"),
            P(("row", "col")),
            P("row", "col"),
            P("col"),
            P(("dp", "row"), "col"),
        ),
        out_specs=(
            P(("dp", "row"), "col"),
            P(("dp", "row"), "col"),
            P("col"),
            P("col"),
            P("col", None, "row"),
            P(None, ("row", "col")),
            P("row", "col"),
            P("col"),
            P("col"),
            P("col"),
            P("col", "row"),
            P(("row", "col")),
            P("row", "col"),
            P("col"),
        ),
        check_vma=False,
    )
```

```python
import functools
import math

import jax
import jax.numpy as jnp
from jax import lax
from jax.experimental import pallas as pl
from jax.experimental.pallas import tpu as pltpu
from jax.sharding import PartitionSpec as P

HD = 64
HEADS = 16
LONGEST = 512
BLOCK = 256

epsilon = 1e-05
masked = -1e30
GROUP = ("row", "col")
VMEM_LIMIT = 48 * 1024 * 1024


def gelu_tanh(values):
    return jax.nn.gelu(values, approximate=True)


def norm_stats(values):
    mean = jnp.mean(values, axis=-1, keepdims=True)
    away = values - mean
    inverse = lax.rsqrt(jnp.mean(away * away, axis=-1, keepdims=True) + epsilon)
    return away * inverse, inverse


def norm_apply(centred, gain, shift):
    normed = centred * gain.astype(jnp.float32) + shift.astype(jnp.float32)
    return normed.astype(jnp.bfloat16)


def norm_backward(upstream, centred, inverse, gain):
    scaled = upstream * gain.astype(jnp.float32)
    total = jnp.mean(scaled, axis=-1, keepdims=True)
    mixed = jnp.mean(scaled * centred, axis=-1, keepdims=True)
    back = inverse * (scaled - total - centred * mixed)
    return (back, jnp.sum(upstream * centred, axis=0), jnp.sum(upstream, axis=0))


def product(left, right):
    return jnp.dot(left, right, preferred_element_type=jnp.float32)


def product_flip(left, right):
    return lax.dot_general(left, right, (((1,), (1,)), ((), ())), preferred_element_type=jnp.float32)


def outer_sum(left, right):
    return lax.dot_general(left, right, (((0,), (0,)), ((), ())), preferred_element_type=jnp.float32)


def head_parts(q_ref, k_ref, v_ref, first, slope, head, start, begin, window, scale):
    lanes = slice(head * HD, (head + 1) * HD)
    query = q_ref[pl.ds(start, BLOCK), lanes]
    keys = k_ref[pl.ds(begin, window), lanes]
    values = v_ref[pl.ds(begin, window), lanes]
    scores = product_flip(query, keys) * scale
    rows_at = start + lax.broadcasted_iota(jnp.int32, (BLOCK, window), 0)
    keys_at = begin + lax.broadcasted_iota(jnp.int32, (BLOCK, window), 1)
    distance = keys_at - rows_at
    scores = scores + slope * distance.astype(jnp.float32)
    scores = jnp.where((distance <= 0) & (keys_at >= first), scores, masked)
    peak = jnp.max(scores, axis=-1, keepdims=True)
    spread = jnp.exp(scores - peak)
    total = jnp.sum(spread, axis=-1, keepdims=True)
    return query, keys, values, spread * (1.0 / total)


def attend_kernel(heads, window, scale, slopes_ref, first_ref, q_ref, k_ref, v_ref, out_ref):
    start = pl.multiple_of(pl.program_id(0) * BLOCK, BLOCK)
    begin = pl.multiple_of(jnp.maximum(start + BLOCK - window, 0), BLOCK)
    first = first_ref[pl.ds(start, BLOCK), :]
    parts = []
    for head in range(heads):
        _, _, values, probability = head_parts(
            q_ref, k_ref, v_ref, first, slopes_ref[head], head, start, begin, window, scale
        )
        parts.append(product(probability.astype(jnp.bfloat16), values))
    out_ref[pl.ds(start, BLOCK), :] = jnp.concatenate(parts, axis=1).astype(jnp.bfloat16)


def attend_back_kernel(
    heads, window, scale, slopes_ref, first_ref, q_ref, k_ref, v_ref, up_ref, out_ref, dk_ref, dv_ref
):
    step = pl.program_id(0)

    @pl.when(step == 0)
    def _():
        dk_ref[...] = jnp.zeros_like(dk_ref)
        dv_ref[...] = jnp.zeros_like(dv_ref)

    start = pl.multiple_of(step * BLOCK, BLOCK)
    begin = pl.multiple_of(jnp.maximum(start + BLOCK - window, 0), BLOCK)
    first = first_ref[pl.ds(start, BLOCK), :]
    grads = []
    key_grads = []
    value_grads = []
    for head in range(heads):
        query, keys, values, probability = head_parts(
            q_ref, k_ref, v_ref, first, slopes_ref[head], head, start, begin, window, scale
        )
        above = up_ref[pl.ds(start, BLOCK), head * HD : (head + 1) * HD]
        grad_prob = product_flip(above, values)
        centre = jnp.sum(probability * grad_prob, axis=-1, keepdims=True)
        grad_scores = (probability * (grad_prob - centre)).astype(jnp.bfloat16)
        grads.append(product(grad_scores, keys) * scale)
        key_grads.append(outer_sum(grad_scores, query) * scale)
        value_grads.append(outer_sum(probability.astype(jnp.bfloat16), above))
    width = heads * HD
    out_ref[pl.ds(start, BLOCK), 0:width] = jnp.concatenate(grads, axis=1).astype(jnp.bfloat16)
    dk_ref[pl.ds(begin, window), :] += jnp.concatenate(key_grads, axis=1)
    dv_ref[pl.ds(begin, window), :] += jnp.concatenate(value_grads, axis=1)

    @pl.when(step == pl.num_programs(0) - 1)
    def _():
        out_ref[:, width : 2 * width] = dk_ref[...].astype(jnp.bfloat16)
        out_ref[:, 2 * width : 3 * width] = dv_ref[...].astype(jnp.bfloat16)


def attention_specs(count, width):
    whole = pl.BlockSpec((count, width), lambda i: (0, 0))
    return [
        pl.BlockSpec(memory_space=pltpu.SMEM),
        pl.BlockSpec((count, 1), lambda i: (0, 0)),
        pl.BlockSpec((count, width), lambda i: (0, 0)),
        pl.BlockSpec((count, width), lambda i: (0, 1)),
        pl.BlockSpec((count, width), lambda i: (0, 2)),
    ], whole


def attend(projected, first, slopes, scale):
    count = projected.shape[0]
    width = projected.shape[1] // 3
    heads = width // HD
    window = min(LONGEST + BLOCK, count)
    specs, whole = attention_specs(count, width)
    area = heads * count * window
    return pl.pallas_call(
        functools.partial(attend_kernel, heads, window, scale),
        grid=(count // BLOCK,),
        in_specs=specs,
        out_specs=whole,
        out_shape=jax.ShapeDtypeStruct((count, width), jnp.bfloat16),
        compiler_params=pltpu.CompilerParams(vmem_limit_bytes=VMEM_LIMIT),
        cost_estimate=pl.CostEstimate(
            flops=4 * area * HD, bytes_accessed=8 * count * width, transcendentals=area
        ),
        name="attend",
    )(slopes, first, projected, projected, projected)


def attend_back(projected, first, slopes, scale, upstream):
    count = projected.shape[0]
    width = projected.shape[1] // 3
    heads = width // HD
    window = min(LONGEST + BLOCK, count)
    specs, whole = attention_specs(count, width)
    area = heads * count * window
    return pl.pallas_call(
        functools.partial(attend_back_kernel, heads, window, scale),
        grid=(count // BLOCK,),
        in_specs=specs + [whole],
        out_specs=pl.BlockSpec((count, 3 * width), lambda i: (0, 0)),
        out_shape=jax.ShapeDtypeStruct((count, 3 * width), jnp.bfloat16),
        scratch_shapes=[pltpu.VMEM((count, width), jnp.float32)] * 2,
        compiler_params=pltpu.CompilerParams(vmem_limit_bytes=VMEM_LIMIT),
        cost_estimate=pl.CostEstimate(
            flops=10 * area * HD, bytes_accessed=14 * count * width, transcendentals=area
        ),
        name="attend_back",
    )(slopes, first, projected, projected, projected, upstream)


MESH = pl.DeviceIdType.MESH
MOVE = pl.CostEstimate(flops=0, bytes_accessed=64 * 1024 * 1024, transcendentals=0)
ROWS = 2
COLS = 4


def positions():
    row = lax.axis_index("row")
    col = lax.axis_index("col")
    return row, col, 1 - row, lax.rem(col + 2, COLS), col + 1 - 2 * lax.rem(col, 2)


def greet(devices):
    barrier = pltpu.get_barrier_semaphore()
    for device in devices:
        pl.semaphore_signal(barrier, inc=1, device_id=device, device_id_type=MESH)
    pl.semaphore_wait(barrier, len(devices))


def remote(source, target, send_sem, recv_sem, device):
    return pltpu.make_async_remote_copy(
        src_ref=source,
        dst_ref=target,
        send_sem=send_sem,
        recv_sem=recv_sem,
        device_id=device,
        device_id_type=MESH,
    )


GATHER_COPIES = 11


def gather_kernel(tiled, total, *refs):
    ins = refs[:total]
    outs = refs[total : 2 * total]
    local_sem, send_sem, recv_sem = refs[2 * total :]
    row, col, other_row, other_col, twin = positions()
    side, over, core = {"row": other_row}, {"col": other_col}, {"col": twin}
    greet([side, over, core])
    copies = []
    locals_ = []
    for which in range(total):
        block, out = ins[which], outs[which]
        count, width = block.shape
        half = count // 2

        def place(r, c, low, size, out=out, count=count, width=width):
            if tiled:
                at = pl.multiple_of(c * width, width)
                return out.at[pl.ds(pl.multiple_of(r * count, count) + low, size), pl.ds(at, width)]
            at = pl.multiple_of((r * COLS + c) * count, count)
            return out.at[pl.ds(at + low, size), :]

        def mine(low, size, block=block):
            return block.at[pl.ds(low, size), :]

        def one(index, source, target, device, base=which * GATHER_COPIES):
            return remote(source, target, send_sem.at[base + index], recv_sem.at[base + index], device)

        def relay(index, r, c, low, size, device):
            return one(index, place(r, c, low, size), place(r, c, low, size), device)

        copies.append(
            [
                one(0, mine(0, half), place(row, col, 0, half), side),
                one(1, mine(half, half), place(row, col, half, half), over),
                one(2, mine(half, half), place(row, col, half, half), side),
                one(3, mine(0, half), place(row, col, 0, half), over),
                one(4, mine(0, count), place(row, col, 0, count), core),
                relay(5, other_row, col, 0, half, over),
                relay(6, row, other_col, half, half, side),
                relay(7, other_row, col, 0, count, core),
                relay(8, row, other_col, 0, count, core),
                relay(9, other_row, other_col, 0, half, core),
                relay(10, other_row, other_col, half, half, core),
            ]
        )
        locals_.append(
            pltpu.make_async_copy(block, place(row, col, 0, count), local_sem.at[which])
        )
        for index in range(5):
            copies[which][index].start()
        locals_[which].start()
    for which in range(total):
        group = copies[which]
        group[0].wait_recv()
        group[5].start()
        group[1].wait_recv()
        group[6].start()
        group[2].wait_recv()
        group[7].start()
        group[3].wait_recv()
        group[8].start()
    for which in range(total):
        group = copies[which]
        group[5].wait_recv()
        group[9].start()
        group[6].wait_recv()
        group[10].start()
    for which in range(total):
        for index in (4, 7, 8, 9, 10):
            copies[which][index].wait_recv()
        for index in range(GATHER_COPIES):
            copies[which][index].wait_send()
        locals_[which].wait()


def gather_group(shards, tiled, collective_id):
    total = len(shards)
    shapes = []
    for shard in shards:
        count, width = shard.shape
        shape = (ROWS * count, COLS * width) if tiled else (ROWS * COLS * count, width)
        shapes.append(jax.ShapeDtypeStruct(shape, shard.dtype))
    return pl.pallas_call(
        functools.partial(gather_kernel, tiled, total),
        in_specs=[pl.BlockSpec(memory_space=pltpu.VMEM)] * total,
        out_specs=[pl.BlockSpec(memory_space=pltpu.VMEM)] * total,
        out_shape=shapes,
        scratch_shapes=[
            pltpu.SemaphoreType.DMA((total,)),
            pltpu.SemaphoreType.DMA((total * GATHER_COPIES,)),
            pltpu.SemaphoreType.DMA((total * GATHER_COPIES,)),
        ],
        compiler_params=pltpu.CompilerParams(
            collective_id=collective_id, has_side_effects=True, vmem_limit_bytes=VMEM_LIMIT
        ),
        cost_estimate=MOVE,
        name="gather_group",
    )(*shards)


def scatter_kernel(part_ref, out_ref, pair, work, from_side, from_over, last, passed, send_sem, recv_sem):
    own = out_ref.shape[0]
    half = own // 2
    row, col, other_row, other_col, twin = positions()
    side, over, core = {"row": other_row}, {"col": other_col}, {"col": twin}
    other_twin = lax.rem(twin + 2, COLS)
    low, high = pl.ds(0, half), pl.ds(half, half)
    keep = [(other_row, other_col), (other_row, col), (row, other_col), (row, col)]
    give = [(other_row, other_twin), (other_row, twin), (row, other_twin), (row, twin)]

    def piece(r, c):
        return part_ref.at[pl.ds(pl.multiple_of((r * COLS + c) * own, own), own), :]

    def one(index, source, target, device):
        return remote(source, target, send_sem.at[index], recv_sem.at[index], device)

    greet([side, over, core])
    first = [one(chip, piece(*give[chip]), pair.at[chip], core) for chip in range(4)]
    for copy in first:
        copy.start()
    diag_side = one(4, work.at[0, low], from_side.at[0], side)
    near_side = one(5, work.at[1, low], from_side.at[1], side)
    diag_over = one(6, work.at[0, high], from_over.at[0], over)
    near_over = one(7, work.at[2, high], from_over.at[1], over)
    last_over = one(8, passed.at[0], last.at[0], over)
    last_side = one(9, passed.at[1], last.at[1], side)

    def add_pair(chip):
        first[chip].wait_recv()
        kept = piece(*keep[chip])[...].astype(jnp.float32)
        work[chip] = (kept + pair[chip].astype(jnp.float32)).astype(jnp.bfloat16)

    add_pair(0)
    diag_side.start()
    diag_over.start()
    add_pair(1)
    near_side.start()
    add_pair(2)
    near_over.start()
    add_pair(3)
    diag_side.wait_recv()
    passed[0] = (work[2, low].astype(jnp.float32) + from_side[0].astype(jnp.float32)).astype(
        jnp.bfloat16
    )
    last_over.start()
    diag_over.wait_recv()
    passed[1] = (work[1, high].astype(jnp.float32) + from_over[0].astype(jnp.float32)).astype(
        jnp.bfloat16
    )
    last_side.start()
    near_side.wait_recv()
    out_ref[low, :] = work[3, low].astype(jnp.float32) + from_side[1].astype(jnp.float32)
    near_over.wait_recv()
    out_ref[high, :] = work[3, high].astype(jnp.float32) + from_over[1].astype(jnp.float32)
    last_over.wait_recv()
    out_ref[low, :] += last[0].astype(jnp.float32)
    last_side.wait_recv()
    out_ref[high, :] += last[1].astype(jnp.float32)
    for copy in first + [diag_side, near_side, diag_over, near_over, last_over, last_side]:
        copy.wait_send()


def scatter_group(partial_sum):
    count, width = partial_sum.shape
    own = count // (ROWS * COLS)
    half = own // 2
    return pl.pallas_call(
        scatter_kernel,
        in_specs=[pl.BlockSpec(memory_space=pltpu.VMEM)],
        out_specs=pl.BlockSpec(memory_space=pltpu.VMEM),
        out_shape=jax.ShapeDtypeStruct((own, width), jnp.float32),
        scratch_shapes=[
            pltpu.VMEM((4, own, width), jnp.bfloat16),
            pltpu.VMEM((4, own, width), jnp.bfloat16),
            pltpu.VMEM((2, half, width), jnp.bfloat16),
            pltpu.VMEM((2, half, width), jnp.bfloat16),
            pltpu.VMEM((2, half, width), jnp.bfloat16),
            pltpu.VMEM((2, half, width), jnp.bfloat16),
            pltpu.SemaphoreType.DMA((10,)),
            pltpu.SemaphoreType.DMA((10,)),
        ],
        compiler_params=pltpu.CompilerParams(
            collective_id=2, has_side_effects=True, vmem_limit_bytes=VMEM_LIMIT
        ),
        cost_estimate=MOVE,
        name="scatter_group",
    )(partial_sum.astype(jnp.bfloat16))


def exchange_copies(plan, ins, outs, local_sem, send_sem, recv_sem):
    col = lax.axis_index("col")
    copies = []
    locals_ = []
    index = 0
    local = 0
    for kind, groups, source, target in zip(*zip(*plan), ins, outs):
        for group in range(groups):
            for step in range(COLS):
                peer = lax.rem(col + step, COLS)
                if kind == "columns":
                    rows, width = source.shape[0], target.shape[1] // groups
                    away = pl.multiple_of((group * COLS + peer) * width, width)
                    block = source.at[:, pl.ds(away, width)]
                    slot = target.at[
                        pl.ds(pl.multiple_of(col * rows, rows), rows), pl.ds(group * width, width)
                    ]
                else:
                    rows, width = target.shape[0], source.shape[1] // groups
                    away = pl.multiple_of(peer * rows, rows)
                    block = source.at[pl.ds(away, rows), pl.ds(group * width, width)]
                    slot = target.at[
                        :, pl.ds(pl.multiple_of((group * COLS + col) * width, width), width)
                    ]
                if step == 0:
                    locals_.append(pltpu.make_async_copy(block, slot, local_sem.at[local]))
                    local += 1
                else:
                    copies.append(
                        remote(block, slot, send_sem.at[index], recv_sem.at[index], {"col": peer})
                    )
                    index += 1
    return copies, locals_


def greet_columns():
    col = lax.axis_index("col")
    greet([{"col": lax.rem(col + step, COLS)} for step in range(1, COLS)])


def exchange_kernel(plan, *refs):
    total = len(plan)
    greet_columns()
    copies, locals_ = exchange_copies(plan, refs[:total], refs[total : 2 * total], *refs[2 * total :])
    for copy in copies + locals_:
        copy.start()
    for copy in copies + locals_:
        copy.wait()


def exchange_shapes(arrays, plan):
    shapes = []
    for array, (kind, _) in zip(arrays, plan):
        rows, width = array.shape
        shape = (rows * COLS, width // COLS) if kind == "columns" else (rows // COLS, width * COLS)
        shapes.append(jax.ShapeDtypeStruct(shape, array.dtype))
    blocks = sum(groups for _, groups in plan)
    scratch = [
        pltpu.SemaphoreType.DMA((blocks,)),
        pltpu.SemaphoreType.DMA((blocks * (COLS - 1),)),
        pltpu.SemaphoreType.DMA((blocks * (COLS - 1),)),
    ]
    return shapes, scratch


def exchange(arrays, plan, collective_id):
    shapes, scratch = exchange_shapes(arrays, plan)
    return pl.pallas_call(
        functools.partial(exchange_kernel, plan),
        in_specs=[pl.BlockSpec(memory_space=pl.ANY)] * len(arrays),
        out_specs=[pl.BlockSpec(memory_space=pl.ANY)] * len(arrays),
        out_shape=shapes,
        scratch_shapes=scratch,
        compiler_params=pltpu.CompilerParams(
            collective_id=collective_id, has_side_effects=True, vmem_limit_bytes=VMEM_LIMIT
        ),
        cost_estimate=MOVE,
        name="exchange",
    )(*arrays)


def total_kernel(groups, block_ref, out_ref, slots, local_sem, send_sem, recv_sem):
    total = groups * ROWS
    here = lax.axis_index("dp") * ROWS + lax.axis_index("row")
    peers = []
    for step in range(1, total):
        peer = lax.rem(here + step, total)
        peers.append({"dp": lax.div(peer, ROWS), "row": lax.rem(peer, ROWS)})
    greet(peers)
    own = pltpu.make_async_copy(block_ref, slots.at[here], local_sem)
    own.start()
    copies = [
        remote(block_ref, slots.at[here], send_sem.at[index], recv_sem.at[index], peer)
        for index, peer in enumerate(peers)
    ]
    for copy in copies:
        copy.start()
    own.wait()
    for copy in copies:
        copy.wait()
    half = block_ref.shape[0] // 2
    row = lax.axis_index("row")
    upper = slots[0, :half]
    for index in range(1, total):
        upper = upper + slots[index, :half]
    lower = slots[row, half:]
    for index in range(1, groups):
        lower = lower + slots[index * ROWS + row, half:]
    out_ref[:half] = upper
    out_ref[half:] = lower


def total_over_rows(block):
    groups = lax.axis_size("dp")
    others = groups * ROWS - 1
    return pl.pallas_call(
        functools.partial(total_kernel, groups),
        in_specs=[pl.BlockSpec(memory_space=pltpu.VMEM)],
        out_specs=pl.BlockSpec(memory_space=pltpu.VMEM),
        out_shape=jax.ShapeDtypeStruct(block.shape, block.dtype),
        scratch_shapes=[
            pltpu.VMEM((groups * ROWS, *block.shape), block.dtype),
            pltpu.SemaphoreType.DMA,
            pltpu.SemaphoreType.DMA((others,)),
            pltpu.SemaphoreType.DMA((others,)),
        ],
        compiler_params=pltpu.CompilerParams(
            collective_id=7, has_side_effects=True, vmem_limit_bytes=VMEM_LIMIT
        ),
        name="total_over_rows",
    )(block)


def after(array, *others):
    return lax.optimization_barrier((array, *others))[0]


def on_device(
    tokens,
    lengths,
    ln1_gain,
    ln1_bias,
    qkv_weight,
    qv_bias,
    out_weight,
    out_bias,
    ln2_gain,
    ln2_bias,
    up_weight,
    up_bias,
    down_weight,
    down_bias,
    cotangent,
):
    cols = lax.axis_size("col")
    rows = lax.axis_size("row")
    count = tokens.shape[0] * rows
    own = count // (rows * cols)
    place = lax.axis_index("row") * cols + lax.axis_index("col")
    local_heads = qkv_weight.shape[2] // cols // HD
    first_head = place * local_heads
    slopes = jnp.exp2(
        -8.0
        * (first_head + jnp.arange(local_heads, dtype=jnp.int32) + 1).astype(jnp.float32)
        / HEADS
    )
    scale = 1.0 / math.sqrt(HD)
    ends = jnp.cumsum(lengths[0])
    starts = ends - lengths[0]
    places = jnp.arange(count, dtype=jnp.int32)
    first = jnp.max(
        jnp.where(starts[None, :] <= places[:, None], starts[None, :], 0), axis=1, keepdims=True
    )

    vectors = jnp.stack([ln1_gain, ln1_bias, out_bias, ln2_gain, ln2_bias, down_bias])
    vectors = lax.all_gather(vectors, "col", axis=1, tiled=True)
    gain_one, shift_one, bias_out, gain_two, shift_two, bias_down = (vectors[i] for i in range(6))

    all_tokens, all_cotangent = gather_group([tokens, cotangent], True, 0)
    qkv_local, out_local, up_local, down_local = exchange(
        [qkv_weight.reshape(qkv_weight.shape[0], -1), out_weight, up_weight, down_weight],
        (("columns", 3), ("rows", 1), ("columns", 1), ("rows", 1)),
        3,
    )

    def mine(array):
        return lax.dynamic_slice_in_dim(array, place * own, own, axis=0)

    centred_all, _ = norm_stats(all_tokens.astype(jnp.float32))
    normed_one = norm_apply(centred_all, gain_one, shift_one)
    residual = mine(all_tokens).astype(jnp.float32)
    upstream = mine(all_cotangent).astype(jnp.float32)
    bias_three = jnp.concatenate([qv_bias[0], jnp.zeros_like(qv_bias[0]), qv_bias[1]])
    projected = (product(normed_one, qkv_local) + bias_three.astype(jnp.float32)).astype(
        jnp.bfloat16
    )
    context = attend(projected, first, slopes, scale)
    attention_out = scatter_group(product(context, out_local))
    middle = residual + attention_out + bias_out.astype(jnp.float32)
    centred_two, inverse_two = norm_stats(middle)
    normed_two = gather_group([norm_apply(centred_two, gain_two, shift_two)], False, 1)[0]
    hidden = product(normed_two, up_local) + up_bias.astype(jnp.float32)
    activated, gelu_pull = jax.vjp(gelu_tanh, hidden)
    activated = activated.astype(jnp.bfloat16)
    grad_active = product_flip(all_cotangent, down_local)
    grad_hidden = gelu_pull(grad_active)[0].astype(jnp.bfloat16)
    grad_up_bias = jnp.sum(grad_hidden.astype(jnp.float32), axis=0)
    grad_up = outer_sum(normed_two, grad_hidden).astype(jnp.bfloat16)
    grad_down = outer_sum(activated, all_cotangent).astype(jnp.bfloat16)
    grad_up, grad_down = exchange([grad_up, grad_down], (("rows", 1), ("columns", 1)), 4)
    grad_up_weight, grad_down_weight = lax.psum((grad_up, grad_down), "dp")
    partial_two = product_flip(grad_hidden, up_local).astype(jnp.bfloat16)
    grad_normed_two = scatter_group(after(partial_two, grad_up, grad_down))
    grad_down_bias = jnp.sum(upstream, axis=0)

    back_two, grad_ln2_gain, grad_ln2_bias = norm_backward(
        grad_normed_two, centred_two, inverse_two, gain_two
    )
    grad_middle = upstream + back_two
    grad_out_bias = jnp.sum(grad_middle, axis=0)
    grad_attention = gather_group([grad_middle.astype(jnp.bfloat16)], False, 1)[0]
    grad_context = product_flip(grad_attention, out_local).astype(jnp.bfloat16)
    grad_out = outer_sum(context, grad_attention).astype(jnp.bfloat16)
    grad_projected = attend_back(projected, first, slopes, scale, grad_context)
    summed = jnp.sum(grad_projected.astype(jnp.float32), axis=0).reshape(3, -1)
    grad_qv_bias = jnp.stack([summed[0], summed[2]])
    grad_qkv = outer_sum(normed_one, grad_projected).astype(jnp.bfloat16)
    grad_out, grad_qkv = exchange([grad_out, grad_qkv], (("columns", 1), ("rows", 3)), 5)
    sent_out, sent_qkv, grad_up_weight, grad_down_weight = lax.optimization_barrier(
        (grad_out, grad_qkv, grad_up_weight, grad_down_weight)
    )
    grad_out_weight, grad_qkv_weight = lax.psum((sent_out, sent_qkv), "dp")
    partial_one = product_flip(grad_projected, qkv_local).astype(jnp.bfloat16)
    grad_normed_one = scatter_group(after(partial_one, sent_out, sent_qkv))

    partial_feed = product(activated, down_local).astype(jnp.bfloat16)
    feed_out = scatter_group(after(partial_feed, grad_normed_one))
    block_out = (middle + feed_out + bias_down.astype(jnp.float32)).astype(jnp.bfloat16)

    centred_one, inverse_one = norm_stats(residual)
    back_one, grad_ln1_gain, grad_ln1_bias = norm_backward(
        grad_normed_one, centred_one, inverse_one, gain_one
    )
    grad_tokens = grad_middle + back_one

    width = local_heads * HD
    spare = jnp.zeros_like(grad_out_bias)
    vectors = jnp.stack(
        [
            grad_ln1_gain,
            grad_ln1_bias,
            grad_out_bias,
            grad_ln2_gain,
            grad_ln2_bias,
            grad_down_bias,
            spare,
            spare,
        ]
    )
    block_out, grad_tokens, vectors = exchange(
        [block_out, grad_tokens.astype(jnp.bfloat16), vectors], (("columns", 1),) * 3, 6
    )
    features = tokens.shape[1]
    biases = jnp.concatenate([grad_qv_bias.reshape(-1), grad_up_bias])
    biases = jnp.pad(biases, (0, 8 * features - biases.shape[0])).reshape(8, features)
    vector_sums = total_over_rows(
        jnp.concatenate([jnp.sum(vectors.reshape(cols, 8, -1), axis=0), biases])
    )
    biases = vector_sums[8:].reshape(-1)
    return (
        block_out,
        grad_tokens.astype(jnp.float32),
        vector_sums[0],
        vector_sums[1],
        grad_qkv_weight.astype(jnp.float32).reshape(qkv_weight.shape),
        biases[: 2 * width].reshape(2, width),
        grad_out_weight.astype(jnp.float32),
        vector_sums[2],
        vector_sums[3],
        vector_sums[4],
        grad_up_weight.astype(jnp.float32),
        biases[2 * width : 2 * width + up_bias.shape[0]],
        grad_down_weight.astype(jnp.float32),
        vector_sums[5],
    )


def solution(mesh):
    return jax.shard_map(
        on_device,
        mesh=mesh,
        in_specs=(
            P(("dp", "row"), "col"),
            P("dp", None),
            P("col"),
            P("col"),
            P("col", None, "row"),
            P(None, ("row", "col")),
            P("row", "col"),
            P("col"),
            P("col"),
            P("col"),
            P("col", "row"),
            P(("row", "col")),
            P("row", "col"),
            P("col"),
            P(("dp", "row"), "col"),
        ),
        out_specs=(
            P(("dp", "row"), "col"),
            P(("dp", "row"), "col"),
            P("col"),
            P("col"),
            P("col", None, "row"),
            P(None, ("row", "col")),
            P("row", "col"),
            P("col"),
            P("col"),
            P("col"),
            P("col", "row"),
            P(("row", "col")),
            P("row", "col"),
            P("col"),
        ),
        check_vma=False,
    )
```

```python
import functools
import math

import jax
import jax.numpy as jnp
from jax import lax
from jax.experimental import pallas as pl
from jax.experimental.pallas import tpu as pltpu
from jax.sharding import PartitionSpec as P

HD = 64
HEADS = 16
LONGEST = 512
BLOCK = 128

epsilon = 1e-05
masked = -1e30
GROUP = ("row", "col")
VMEM_LIMIT = 48 * 1024 * 1024


def gelu_tanh(values):
    return jax.nn.gelu(values, approximate=True)


def norm_stats(values):
    mean = jnp.mean(values, axis=-1, keepdims=True)
    away = values - mean
    inverse = lax.rsqrt(jnp.mean(away * away, axis=-1, keepdims=True) + epsilon)
    return away * inverse, inverse


def norm_apply(centred, gain, shift):
    normed = centred * gain.astype(jnp.float32) + shift.astype(jnp.float32)
    return normed.astype(jnp.bfloat16)


def norm_backward(upstream, centred, inverse, gain):
    scaled = upstream * gain.astype(jnp.float32)
    total = jnp.mean(scaled, axis=-1, keepdims=True)
    mixed = jnp.mean(scaled * centred, axis=-1, keepdims=True)
    back = inverse * (scaled - total - centred * mixed)
    return (back, jnp.sum(upstream * centred, axis=0), jnp.sum(upstream, axis=0))


def product(left, right):
    return jnp.dot(left, right, preferred_element_type=jnp.float32)


def product_flip(left, right):
    return lax.dot_general(left, right, (((1,), (1,)), ((), ())), preferred_element_type=jnp.float32)


def outer_sum(left, right):
    return lax.dot_general(left, right, (((0,), (0,)), ((), ())), preferred_element_type=jnp.float32)


def head_parts(q_ref, k_ref, v_ref, first, slope, head, start, begin, window, scale):
    lanes = slice(head * HD, (head + 1) * HD)
    query = q_ref[pl.ds(start, BLOCK), lanes]
    keys = k_ref[pl.ds(begin, window), lanes]
    values = v_ref[pl.ds(begin, window), lanes]
    scores = product_flip(query, keys) * scale
    rows_at = start + lax.broadcasted_iota(jnp.int32, (BLOCK, window), 0)
    keys_at = begin + lax.broadcasted_iota(jnp.int32, (BLOCK, window), 1)
    distance = keys_at - rows_at
    scores = scores + slope * distance.astype(jnp.float32)
    scores = jnp.where((distance <= 0) & (keys_at >= first), scores, masked)
    peak = jnp.max(scores, axis=-1, keepdims=True)
    spread = jnp.exp(scores - peak)
    total = jnp.sum(spread, axis=-1, keepdims=True)
    return query, keys, values, spread * (1.0 / total)


def attend_kernel(heads, window, scale, slopes_ref, first_ref, q_ref, k_ref, v_ref, out_ref):
    start = pl.multiple_of(pl.program_id(0) * BLOCK, BLOCK)
    begin = pl.multiple_of(jnp.maximum(start + BLOCK - window, 0), BLOCK)
    first = first_ref[pl.ds(start, BLOCK), :]
    parts = []
    for head in range(heads):
        _, _, values, probability = head_parts(
            q_ref, k_ref, v_ref, first, slopes_ref[head], head, start, begin, window, scale
        )
        parts.append(product(probability.astype(jnp.bfloat16), values))
    out_ref[pl.ds(start, BLOCK), :] = jnp.concatenate(parts, axis=1).astype(jnp.bfloat16)


def attend_back_kernel(
    heads, window, scale, slopes_ref, first_ref, q_ref, k_ref, v_ref, up_ref, out_ref, dk_ref, dv_ref
):
    step = pl.program_id(0)

    @pl.when(step == 0)
    def _():
        dk_ref[...] = jnp.zeros_like(dk_ref)
        dv_ref[...] = jnp.zeros_like(dv_ref)

    start = pl.multiple_of(step * BLOCK, BLOCK)
    begin = pl.multiple_of(jnp.maximum(start + BLOCK - window, 0), BLOCK)
    first = first_ref[pl.ds(start, BLOCK), :]
    grads = []
    key_grads = []
    value_grads = []
    for head in range(heads):
        query, keys, values, probability = head_parts(
            q_ref, k_ref, v_ref, first, slopes_ref[head], head, start, begin, window, scale
        )
        above = up_ref[pl.ds(start, BLOCK), head * HD : (head + 1) * HD]
        grad_prob = product_flip(above, values)
        centre = jnp.sum(probability * grad_prob, axis=-1, keepdims=True)
        grad_scores = (probability * (grad_prob - centre)).astype(jnp.bfloat16)
        grads.append(product(grad_scores, keys) * scale)
        key_grads.append(outer_sum(grad_scores, query) * scale)
        value_grads.append(outer_sum(probability.astype(jnp.bfloat16), above))
    width = heads * HD
    out_ref[pl.ds(start, BLOCK), 0:width] = jnp.concatenate(grads, axis=1).astype(jnp.bfloat16)
    dk_ref[pl.ds(begin, window), :] += jnp.concatenate(key_grads, axis=1)
    dv_ref[pl.ds(begin, window), :] += jnp.concatenate(value_grads, axis=1)

    @pl.when(step == pl.num_programs(0) - 1)
    def _():
        out_ref[:, width : 2 * width] = dk_ref[...].astype(jnp.bfloat16)
        out_ref[:, 2 * width : 3 * width] = dv_ref[...].astype(jnp.bfloat16)


def attention_specs(count, width):
    whole = pl.BlockSpec((count, width), lambda i: (0, 0))
    return [
        pl.BlockSpec(memory_space=pltpu.SMEM),
        pl.BlockSpec((count, 1), lambda i: (0, 0)),
        pl.BlockSpec((count, width), lambda i: (0, 0)),
        pl.BlockSpec((count, width), lambda i: (0, 1)),
        pl.BlockSpec((count, width), lambda i: (0, 2)),
    ], whole


def attend(projected, first, slopes, scale):
    count = projected.shape[0]
    width = projected.shape[1] // 3
    heads = width // HD
    window = min(LONGEST + BLOCK, count)
    specs, whole = attention_specs(count, width)
    area = heads * count * window
    return pl.pallas_call(
        functools.partial(attend_kernel, heads, window, scale),
        grid=(count // BLOCK,),
        in_specs=specs,
        out_specs=whole,
        out_shape=jax.ShapeDtypeStruct((count, width), jnp.bfloat16),
        compiler_params=pltpu.CompilerParams(vmem_limit_bytes=VMEM_LIMIT),
        cost_estimate=pl.CostEstimate(
            flops=4 * area * HD, bytes_accessed=8 * count * width, transcendentals=area
        ),
        name="attend",
    )(slopes, first, projected, projected, projected)


def attend_back(projected, first, slopes, scale, upstream):
    count = projected.shape[0]
    width = projected.shape[1] // 3
    heads = width // HD
    window = min(LONGEST + BLOCK, count)
    specs, whole = attention_specs(count, width)
    area = heads * count * window
    return pl.pallas_call(
        functools.partial(attend_back_kernel, heads, window, scale),
        grid=(count // BLOCK,),
        in_specs=specs + [whole],
        out_specs=pl.BlockSpec((count, 3 * width), lambda i: (0, 0)),
        out_shape=jax.ShapeDtypeStruct((count, 3 * width), jnp.bfloat16),
        scratch_shapes=[pltpu.VMEM((count, width), jnp.float32)] * 2,
        compiler_params=pltpu.CompilerParams(vmem_limit_bytes=VMEM_LIMIT),
        cost_estimate=pl.CostEstimate(
            flops=10 * area * HD, bytes_accessed=14 * count * width, transcendentals=area
        ),
        name="attend_back",
    )(slopes, first, projected, projected, projected, upstream)


MESH = pl.DeviceIdType.MESH
MOVE = pl.CostEstimate(flops=0, bytes_accessed=64 * 1024 * 1024, transcendentals=0)
ROWS = 2
COLS = 4


def positions():
    row = lax.axis_index("row")
    col = lax.axis_index("col")
    return row, col, 1 - row, lax.rem(col + 2, COLS), col + 1 - 2 * lax.rem(col, 2)


def greet(devices):
    barrier = pltpu.get_barrier_semaphore()
    for device in devices:
        pl.semaphore_signal(barrier, inc=1, device_id=device, device_id_type=MESH)
    pl.semaphore_wait(barrier, len(devices))


def remote(source, target, send_sem, recv_sem, device):
    return pltpu.make_async_remote_copy(
        src_ref=source,
        dst_ref=target,
        send_sem=send_sem,
        recv_sem=recv_sem,
        device_id=device,
        device_id_type=MESH,
    )


GATHER_COPIES = 11


def gather_kernel(tiled, total, *refs):
    ins = refs[:total]
    outs = refs[total : 2 * total]
    local_sem, send_sem, recv_sem = refs[2 * total :]
    row, col, other_row, other_col, twin = positions()
    side, over, core = {"row": other_row}, {"col": other_col}, {"col": twin}
    greet([side, over, core])
    copies = []
    locals_ = []
    for which in range(total):
        block, out = ins[which], outs[which]
        count, width = block.shape
        half = count // 2

        def place(r, c, low, size, out=out, count=count, width=width):
            if tiled:
                at = pl.multiple_of(c * width, width)
                return out.at[pl.ds(pl.multiple_of(r * count, count) + low, size), pl.ds(at, width)]
            at = pl.multiple_of((r * COLS + c) * count, count)
            return out.at[pl.ds(at + low, size), :]

        def mine(low, size, block=block):
            return block.at[pl.ds(low, size), :]

        def one(index, source, target, device, base=which * GATHER_COPIES):
            return remote(source, target, send_sem.at[base + index], recv_sem.at[base + index], device)

        def relay(index, r, c, low, size, device):
            return one(index, place(r, c, low, size), place(r, c, low, size), device)

        copies.append(
            [
                one(0, mine(0, half), place(row, col, 0, half), side),
                one(1, mine(half, half), place(row, col, half, half), over),
                one(2, mine(half, half), place(row, col, half, half), side),
                one(3, mine(0, half), place(row, col, 0, half), over),
                one(4, mine(0, count), place(row, col, 0, count), core),
                relay(5, other_row, col, 0, half, over),
                relay(6, row, other_col, half, half, side),
                relay(7, other_row, col, 0, count, core),
                relay(8, row, other_col, 0, count, core),
                relay(9, other_row, other_col, 0, half, core),
                relay(10, other_row, other_col, half, half, core),
            ]
        )
        locals_.append(
            pltpu.make_async_copy(block, place(row, col, 0, count), local_sem.at[which])
        )
        for index in range(5):
            copies[which][index].start()
        locals_[which].start()
    for which in range(total):
        group = copies[which]
        group[0].wait_recv()
        group[5].start()
        group[1].wait_recv()
        group[6].start()
        group[2].wait_recv()
        group[7].start()
        group[3].wait_recv()
        group[8].start()
    for which in range(total):
        group = copies[which]
        group[5].wait_recv()
        group[9].start()
        group[6].wait_recv()
        group[10].start()
    for which in range(total):
        for index in (4, 7, 8, 9, 10):
            copies[which][index].wait_recv()
        for index in range(GATHER_COPIES):
            copies[which][index].wait_send()
        locals_[which].wait()


def gather_group(shards, tiled, collective_id):
    total = len(shards)
    shapes = []
    for shard in shards:
        count, width = shard.shape
        shape = (ROWS * count, COLS * width) if tiled else (ROWS * COLS * count, width)
        shapes.append(jax.ShapeDtypeStruct(shape, shard.dtype))
    return pl.pallas_call(
        functools.partial(gather_kernel, tiled, total),
        in_specs=[pl.BlockSpec(memory_space=pltpu.VMEM)] * total,
        out_specs=[pl.BlockSpec(memory_space=pltpu.VMEM)] * total,
        out_shape=shapes,
        scratch_shapes=[
            pltpu.SemaphoreType.DMA((total,)),
            pltpu.SemaphoreType.DMA((total * GATHER_COPIES,)),
            pltpu.SemaphoreType.DMA((total * GATHER_COPIES,)),
        ],
        compiler_params=pltpu.CompilerParams(
            collective_id=collective_id, has_side_effects=True, vmem_limit_bytes=VMEM_LIMIT
        ),
        cost_estimate=MOVE,
        name="gather_group",
    )(*shards)


def scatter_kernel(part_ref, out_ref, pair, work, from_side, from_over, last, passed, send_sem, recv_sem):
    own = out_ref.shape[0]
    half = own // 2
    row, col, other_row, other_col, twin = positions()
    side, over, core = {"row": other_row}, {"col": other_col}, {"col": twin}
    other_twin = lax.rem(twin + 2, COLS)
    low, high = pl.ds(0, half), pl.ds(half, half)
    keep = [(other_row, other_col), (other_row, col), (row, other_col), (row, col)]
    give = [(other_row, other_twin), (other_row, twin), (row, other_twin), (row, twin)]

    def piece(r, c):
        return part_ref.at[pl.ds(pl.multiple_of((r * COLS + c) * own, own), own), :]

    def one(index, source, target, device):
        return remote(source, target, send_sem.at[index], recv_sem.at[index], device)

    greet([side, over, core])
    first = [one(chip, piece(*give[chip]), pair.at[chip], core) for chip in range(4)]
    for copy in first:
        copy.start()
    diag_side = one(4, work.at[0, low], from_side.at[0], side)
    near_side = one(5, work.at[1, low], from_side.at[1], side)
    diag_over = one(6, work.at[0, high], from_over.at[0], over)
    near_over = one(7, work.at[2, high], from_over.at[1], over)
    last_over = one(8, passed.at[0], last.at[0], over)
    last_side = one(9, passed.at[1], last.at[1], side)

    def add_pair(chip):
        first[chip].wait_recv()
        kept = piece(*keep[chip])[...].astype(jnp.float32)
        work[chip] = (kept + pair[chip].astype(jnp.float32)).astype(jnp.bfloat16)

    add_pair(0)
    diag_side.start()
    diag_over.start()
    add_pair(1)
    near_side.start()
    add_pair(2)
    near_over.start()
    add_pair(3)
    diag_side.wait_recv()
    passed[0] = (work[2, low].astype(jnp.float32) + from_side[0].astype(jnp.float32)).astype(
        jnp.bfloat16
    )
    last_over.start()
    diag_over.wait_recv()
    passed[1] = (work[1, high].astype(jnp.float32) + from_over[0].astype(jnp.float32)).astype(
        jnp.bfloat16
    )
    last_side.start()
    near_side.wait_recv()
    out_ref[low, :] = work[3, low].astype(jnp.float32) + from_side[1].astype(jnp.float32)
    near_over.wait_recv()
    out_ref[high, :] = work[3, high].astype(jnp.float32) + from_over[1].astype(jnp.float32)
    last_over.wait_recv()
    out_ref[low, :] += last[0].astype(jnp.float32)
    last_side.wait_recv()
    out_ref[high, :] += last[1].astype(jnp.float32)
    for copy in first + [diag_side, near_side, diag_over, near_over, last_over, last_side]:
        copy.wait_send()


def scatter_group(partial_sum):
    count, width = partial_sum.shape
    own = count // (ROWS * COLS)
    half = own // 2
    return pl.pallas_call(
        scatter_kernel,
        in_specs=[pl.BlockSpec(memory_space=pltpu.VMEM)],
        out_specs=pl.BlockSpec(memory_space=pltpu.VMEM),
        out_shape=jax.ShapeDtypeStruct((own, width), jnp.float32),
        scratch_shapes=[
            pltpu.VMEM((4, own, width), jnp.bfloat16),
            pltpu.VMEM((4, own, width), jnp.bfloat16),
            pltpu.VMEM((2, half, width), jnp.bfloat16),
            pltpu.VMEM((2, half, width), jnp.bfloat16),
            pltpu.VMEM((2, half, width), jnp.bfloat16),
            pltpu.VMEM((2, half, width), jnp.bfloat16),
            pltpu.SemaphoreType.DMA((10,)),
            pltpu.SemaphoreType.DMA((10,)),
        ],
        compiler_params=pltpu.CompilerParams(
            collective_id=2, has_side_effects=True, vmem_limit_bytes=VMEM_LIMIT
        ),
        cost_estimate=MOVE,
        name="scatter_group",
    )(partial_sum.astype(jnp.bfloat16))


def exchange_copies(plan, ins, outs, local_sem, send_sem, recv_sem):
    col = lax.axis_index("col")
    copies = []
    locals_ = []
    index = 0
    local = 0
    for kind, groups, source, target in zip(*zip(*plan), ins, outs):
        for group in range(groups):
            for step in range(COLS):
                peer = lax.rem(col + step, COLS)
                if kind == "columns":
                    rows, width = source.shape[0], target.shape[1] // groups
                    away = pl.multiple_of((group * COLS + peer) * width, width)
                    block = source.at[:, pl.ds(away, width)]
                    slot = target.at[
                        pl.ds(pl.multiple_of(col * rows, rows), rows), pl.ds(group * width, width)
                    ]
                else:
                    rows, width = target.shape[0], source.shape[1] // groups
                    away = pl.multiple_of(peer * rows, rows)
                    block = source.at[pl.ds(away, rows), pl.ds(group * width, width)]
                    slot = target.at[
                        :, pl.ds(pl.multiple_of((group * COLS + col) * width, width), width)
                    ]
                if step == 0:
                    locals_.append(pltpu.make_async_copy(block, slot, local_sem.at[local]))
                    local += 1
                else:
                    copies.append(
                        remote(block, slot, send_sem.at[index], recv_sem.at[index], {"col": peer})
                    )
                    index += 1
    return copies, locals_


def greet_columns():
    col = lax.axis_index("col")
    greet([{"col": lax.rem(col + step, COLS)} for step in range(1, COLS)])


def exchange_kernel(plan, *refs):
    total = len(plan)
    greet_columns()
    copies, locals_ = exchange_copies(plan, refs[:total], refs[total : 2 * total], *refs[2 * total :])
    for copy in copies + locals_:
        copy.start()
    for copy in copies + locals_:
        copy.wait()


def exchange_shapes(arrays, plan):
    shapes = []
    for array, (kind, _) in zip(arrays, plan):
        rows, width = array.shape
        shape = (rows * COLS, width // COLS) if kind == "columns" else (rows // COLS, width * COLS)
        shapes.append(jax.ShapeDtypeStruct(shape, array.dtype))
    blocks = sum(groups for _, groups in plan)
    scratch = [
        pltpu.SemaphoreType.DMA((blocks,)),
        pltpu.SemaphoreType.DMA((blocks * (COLS - 1),)),
        pltpu.SemaphoreType.DMA((blocks * (COLS - 1),)),
    ]
    return shapes, scratch


def exchange(arrays, plan, collective_id):
    shapes, scratch = exchange_shapes(arrays, plan)
    return pl.pallas_call(
        functools.partial(exchange_kernel, plan),
        in_specs=[pl.BlockSpec(memory_space=pl.ANY)] * len(arrays),
        out_specs=[pl.BlockSpec(memory_space=pl.ANY)] * len(arrays),
        out_shape=shapes,
        scratch_shapes=scratch,
        compiler_params=pltpu.CompilerParams(
            collective_id=collective_id, has_side_effects=True, vmem_limit_bytes=VMEM_LIMIT
        ),
        cost_estimate=MOVE,
        name="exchange",
    )(*arrays)


def total_kernel(groups, block_ref, out_ref, slots, local_sem, send_sem, recv_sem):
    total = groups * ROWS
    here = lax.axis_index("dp") * ROWS + lax.axis_index("row")
    peers = []
    for step in range(1, total):
        peer = lax.rem(here + step, total)
        peers.append({"dp": lax.div(peer, ROWS), "row": lax.rem(peer, ROWS)})
    greet(peers)
    own = pltpu.make_async_copy(block_ref, slots.at[here], local_sem)
    own.start()
    copies = [
        remote(block_ref, slots.at[here], send_sem.at[index], recv_sem.at[index], peer)
        for index, peer in enumerate(peers)
    ]
    for copy in copies:
        copy.start()
    own.wait()
    for copy in copies:
        copy.wait()
    half = block_ref.shape[0] // 2
    row = lax.axis_index("row")
    upper = slots[0, :half]
    for index in range(1, total):
        upper = upper + slots[index, :half]
    lower = slots[row, half:]
    for index in range(1, groups):
        lower = lower + slots[index * ROWS + row, half:]
    out_ref[:half] = upper
    out_ref[half:] = lower


def total_over_rows(block):
    groups = lax.axis_size("dp")
    others = groups * ROWS - 1
    return pl.pallas_call(
        functools.partial(total_kernel, groups),
        in_specs=[pl.BlockSpec(memory_space=pltpu.VMEM)],
        out_specs=pl.BlockSpec(memory_space=pltpu.VMEM),
        out_shape=jax.ShapeDtypeStruct(block.shape, block.dtype),
        scratch_shapes=[
            pltpu.VMEM((groups * ROWS, *block.shape), block.dtype),
            pltpu.SemaphoreType.DMA,
            pltpu.SemaphoreType.DMA((others,)),
            pltpu.SemaphoreType.DMA((others,)),
        ],
        compiler_params=pltpu.CompilerParams(
            collective_id=7, has_side_effects=True, vmem_limit_bytes=VMEM_LIMIT
        ),
        name="total_over_rows",
    )(block)


def after(array, *others):
    return lax.optimization_barrier((array, *others))[0]


def on_device(
    tokens,
    lengths,
    ln1_gain,
    ln1_bias,
    qkv_weight,
    qv_bias,
    out_weight,
    out_bias,
    ln2_gain,
    ln2_bias,
    up_weight,
    up_bias,
    down_weight,
    down_bias,
    cotangent,
):
    cols = lax.axis_size("col")
    rows = lax.axis_size("row")
    count = tokens.shape[0] * rows
    own = count // (rows * cols)
    place = lax.axis_index("row") * cols + lax.axis_index("col")
    local_heads = qkv_weight.shape[2] // cols // HD
    first_head = place * local_heads
    slopes = jnp.exp2(
        -8.0
        * (first_head + jnp.arange(local_heads, dtype=jnp.int32) + 1).astype(jnp.float32)
        / HEADS
    )
    scale = 1.0 / math.sqrt(HD)
    ends = jnp.cumsum(lengths[0])
    starts = ends - lengths[0]
    places = jnp.arange(count, dtype=jnp.int32)
    first = jnp.max(
        jnp.where(starts[None, :] <= places[:, None], starts[None, :], 0), axis=1, keepdims=True
    )

    vectors = jnp.stack([ln1_gain, ln1_bias, out_bias, ln2_gain, ln2_bias, down_bias])
    vectors = lax.all_gather(vectors, "col", axis=1, tiled=True)
    gain_one, shift_one, bias_out, gain_two, shift_two, bias_down = (vectors[i] for i in range(6))

    all_tokens, all_cotangent = gather_group([tokens, cotangent], True, 0)
    qkv_local, out_local, up_local, down_local = exchange(
        [qkv_weight.reshape(qkv_weight.shape[0], -1), out_weight, up_weight, down_weight],
        (("columns", 3), ("rows", 1), ("columns", 1), ("rows", 1)),
        3,
    )

    def mine(array):
        return lax.dynamic_slice_in_dim(array, place * own, own, axis=0)

    centred_all, _ = norm_stats(all_tokens.astype(jnp.float32))
    normed_one = norm_apply(centred_all, gain_one, shift_one)
    residual = mine(all_tokens).astype(jnp.float32)
    upstream = mine(all_cotangent).astype(jnp.float32)
    bias_three = jnp.concatenate([qv_bias[0], jnp.zeros_like(qv_bias[0]), qv_bias[1]])
    projected = (product(normed_one, qkv_local) + bias_three.astype(jnp.float32)).astype(
        jnp.bfloat16
    )
    context = attend(projected, first, slopes, scale)
    attention_out = scatter_group(product(context, out_local))
    middle = residual + attention_out + bias_out.astype(jnp.float32)
    centred_two, inverse_two = norm_stats(middle)
    normed_two = gather_group([norm_apply(centred_two, gain_two, shift_two)], False, 1)[0]
    hidden = product(normed_two, up_local) + up_bias.astype(jnp.float32)
    activated, gelu_pull = jax.vjp(gelu_tanh, hidden)
    activated = activated.astype(jnp.bfloat16)
    grad_active = product_flip(all_cotangent, down_local)
    grad_hidden = gelu_pull(grad_active)[0].astype(jnp.bfloat16)
    grad_up_bias = jnp.sum(grad_hidden.astype(jnp.float32), axis=0)
    grad_up = outer_sum(normed_two, grad_hidden).astype(jnp.bfloat16)
    grad_down = outer_sum(activated, all_cotangent).astype(jnp.bfloat16)
    grad_up, grad_down = exchange([grad_up, grad_down], (("rows", 1), ("columns", 1)), 4)
    grad_up_weight, grad_down_weight = lax.psum((grad_up, grad_down), "dp")
    partial_two = product_flip(grad_hidden, up_local).astype(jnp.bfloat16)
    grad_normed_two = scatter_group(after(partial_two, grad_up, grad_down))
    grad_down_bias = jnp.sum(upstream, axis=0)

    back_two, grad_ln2_gain, grad_ln2_bias = norm_backward(
        grad_normed_two, centred_two, inverse_two, gain_two
    )
    grad_middle = upstream + back_two
    grad_out_bias = jnp.sum(grad_middle, axis=0)
    grad_attention = gather_group([grad_middle.astype(jnp.bfloat16)], False, 1)[0]
    grad_context = product_flip(grad_attention, out_local).astype(jnp.bfloat16)
    grad_out = outer_sum(context, grad_attention).astype(jnp.bfloat16)
    grad_projected = attend_back(projected, first, slopes, scale, grad_context)
    summed = jnp.sum(grad_projected.astype(jnp.float32), axis=0).reshape(3, -1)
    grad_qv_bias = jnp.stack([summed[0], summed[2]])
    grad_qkv = outer_sum(normed_one, grad_projected).astype(jnp.bfloat16)
    grad_out, grad_qkv = exchange([grad_out, grad_qkv], (("columns", 1), ("rows", 3)), 5)
    sent_out, sent_qkv, grad_up_weight, grad_down_weight = lax.optimization_barrier(
        (grad_out, grad_qkv, grad_up_weight, grad_down_weight)
    )
    grad_out_weight, grad_qkv_weight = lax.psum((sent_out, sent_qkv), "dp")
    partial_one = product_flip(grad_projected, qkv_local).astype(jnp.bfloat16)
    grad_normed_one = scatter_group(after(partial_one, sent_out, sent_qkv))

    partial_feed = product(activated, down_local).astype(jnp.bfloat16)
    feed_out = scatter_group(after(partial_feed, grad_normed_one))
    block_out = (middle + feed_out + bias_down.astype(jnp.float32)).astype(jnp.bfloat16)

    centred_one, inverse_one = norm_stats(residual)
    back_one, grad_ln1_gain, grad_ln1_bias = norm_backward(
        grad_normed_one, centred_one, inverse_one, gain_one
    )
    grad_tokens = grad_middle + back_one

    width = local_heads * HD
    spare = jnp.zeros_like(grad_out_bias)
    vectors = jnp.stack(
        [
            grad_ln1_gain,
            grad_ln1_bias,
            grad_out_bias,
            grad_ln2_gain,
            grad_ln2_bias,
            grad_down_bias,
            spare,
            spare,
        ]
    )
    block_out, grad_tokens, vectors = exchange(
        [block_out, grad_tokens.astype(jnp.bfloat16), vectors], (("columns", 1),) * 3, 6
    )
    features = tokens.shape[1]
    biases = jnp.concatenate([grad_qv_bias.reshape(-1), grad_up_bias])
    biases = jnp.pad(biases, (0, 8 * features - biases.shape[0])).reshape(8, features)
    vector_sums = total_over_rows(
        jnp.concatenate([jnp.sum(vectors.reshape(cols, 8, -1), axis=0), biases])
    )
    biases = vector_sums[8:].reshape(-1)
    return (
        block_out,
        grad_tokens.astype(jnp.float32),
        vector_sums[0],
        vector_sums[1],
        grad_qkv_weight.astype(jnp.float32).reshape(qkv_weight.shape),
        biases[: 2 * width].reshape(2, width),
        grad_out_weight.astype(jnp.float32),
        vector_sums[2],
        vector_sums[3],
        vector_sums[4],
        grad_up_weight.astype(jnp.float32),
        biases[2 * width : 2 * width + up_bias.shape[0]],
        grad_down_weight.astype(jnp.float32),
        vector_sums[5],
    )


def solution(mesh):
    return jax.shard_map(
        on_device,
        mesh=mesh,
        in_specs=(
            P(("dp", "row"), "col"),
            P("dp", None),
            P("col"),
            P("col"),
            P("col", None, "row"),
            P(None, ("row", "col")),
            P("row", "col"),
            P("col"),
            P("col"),
            P("col"),
            P("col", "row"),
            P(("row", "col")),
            P("row", "col"),
            P("col"),
            P(("dp", "row"), "col"),
        ),
        out_specs=(
            P(("dp", "row"), "col"),
            P(("dp", "row"), "col"),
            P("col"),
            P("col"),
            P("col", None, "row"),
            P(None, ("row", "col")),
            P("row", "col"),
            P("col"),
            P("col"),
            P("col"),
            P("col", "row"),
            P(("row", "col")),
            P("row", "col"),
            P("col"),
        ),
        check_vma=False,
    )
```
